32 devices in a mesh: row: 4 (over z), col: 8 (over y, x, core).
Axes of the slice: x: 2, y: 2, z: 4, core: 2. Of those that a mesh axis runs over, the one named last changes fastest.
Arguments:
- tokens: bfloat16 [256, 8192], P('row', 'col'), may hold values from -6 to 6
- gate_weight: bfloat16 [8192, 28672], P('col', 'row'), may hold values from -0.09375 to 0.09375
- up_weight: bfloat16 [8192, 28672], P('col', 'row'), may hold values from -0.09375 to 0.09375
- down_weight: bfloat16 [28672, 8192], P('row', 'col'), may hold values from -0.046875 to 0.046875
- gate_keep: int32 [64, 224], P('col', 'row'), may hold values from 0 to 1, as said below
- up_keep: int32 [64, 224], P('col', 'row'), may hold values from 0 to 1, as said below
- down_keep: int32 [224, 64], P('row', 'col'), may hold values from 0 to 1, as said below
Outputs:
- mixed: bfloat16 [256, 8192], P('row', 'col')
The draws below stay inside these ranges and needn't reach their ends.
Inputs may be any that keep to these rules, and one draw needn't show every extreme that they name: `gate_keep`: 1 keeps the block, 0 drops it; the kept share differs between regions of blocks. `up_keep`: 1 keeps the block, 0 drops it; the kept share differs between regions of blocks. `down_keep`: 1 keeps the block, 0 drops it; the kept share differs between regions of blocks.
All inputs are finite; a program needn't handle non-finite values.
Results may differ from the reference program's by a relative error of at most 0.0049.
Values may be sent and summed in bfloat16 or wider, within the bound.
A program may use at most 192 MiB of HBM per device.

```python
import jax
import jax.numpy as jnp

D = 8192
FF = 28672
BLOCK = 128
TOKENS = 256


def keep_blocks(key, rows, cols):
    coarse_rows = (rows + 7) // 8
    coarse_cols = (cols + 7) // 8
    level = jax.random.randint(jax.random.fold_in(key, 11), (coarse_rows, coarse_cols), 1, 8)
    level = jnp.repeat(jnp.repeat(level, 8, axis=0), 8, axis=1)[:rows, :cols]
    values = jax.random.randint(jax.random.fold_in(key, 12), (rows, cols), 0, 8)
    return (values < level).astype(jnp.int32)


def draw_gate_keep(key, part):
    return keep_blocks(jax.random.fold_in(key, 1), D // BLOCK, FF // BLOCK)


def draw_up_keep(key, part):
    return keep_blocks(jax.random.fold_in(key, 2), D // BLOCK, FF // BLOCK)


def draw_down_keep(key, part):
    return keep_blocks(jax.random.fold_in(key, 3), FF // BLOCK, D // BLOCK)


def shard_levels(key, extent, shards, smallest, largest):
    gain, own = 1.0, jax.random.fold_in(key, 6)
    for dim, blocks in shards:
        heights = jnp.exp(jax.random.uniform(jax.random.fold_in(own, dim), (blocks,), jnp.float32, smallest / len(shards), largest / len(shards)))
        gain = gain * jnp.repeat(heights, extent[dim] // blocks).reshape([-1 if axis == dim else 1 for axis in range(len(extent))])
    return gain


def scatter_about(key, extent, width, most, shards=(), held_as=jnp.bfloat16):
    entries = jax.random.normal(key, extent, jnp.float32) * width
    if len(shards) > 0:
        entries = shard_levels(key, extent, shards, -0.22, 0.18) * entries
    return jnp.clip(entries, min=-most, max=most).astype(held_as)


def setup_inputs(seed: int = 0) -> dict:
    key_list = jax.random.split(jax.random.key(seed), 8)
    return {
        "tokens": scatter_about(key_list[0], (TOKENS, D), 1.0, 6.0, ((0, 4), (1, 8))),
        "gate_weight": scatter_about(key_list[1], (D, FF), (D // 2) ** -0.5, 0.09375, ((0, 8), (1, 4))),
        "up_weight": scatter_about(key_list[2], (D, FF), (D // 2) ** -0.5, 0.09375, ((0, 8), (1, 4))),
        "down_weight": scatter_about(key_list[3], (FF, D), (FF // 2) ** -0.5, 0.046875, ((0, 4), (1, 8))),
        "gate_keep": draw_gate_keep(jax.random.fold_in(key_list[7], 71), 0),
        "up_keep": draw_up_keep(jax.random.fold_in(key_list[7], 71), 0),
        "down_keep": draw_down_keep(jax.random.fold_in(key_list[7], 71), 0),
    }


def expand(weight, keep):
    nrow, ncol = keep.shape
    rows, cols = weight.shape
    masked = weight.reshape(nrow, rows // nrow, ncol, cols // ncol) * keep.astype(jnp.bfloat16)[:, None, :, None]
    return masked.reshape(rows, cols)


def reference(tokens, gate_weight, up_weight, down_weight, gate_keep, up_keep, down_keep):
    gate = jnp.dot(tokens, expand(gate_weight, gate_keep), preferred_element_type=jnp.float32)
    up = jnp.dot(tokens, expand(up_weight, up_keep), preferred_element_type=jnp.float32)
    hidden = (jax.nn.silu(gate) * up).astype(jnp.bfloat16)
    return jnp.dot(hidden, expand(down_weight, down_keep), preferred_element_type=jnp.float32).astype(jnp.bfloat16)
```

```python
import functools

import jax
import jax.numpy as jnp
from jax import lax
from jax.experimental import pallas as pl
from jax.experimental.pallas import tpu as pltpu
from jax.sharding import PartitionSpec as P

BLOCK = 128
WIDTH = 512
LAG = 1
SLOTS = 4
MESH = pl.DeviceIdType.MESH


def masked(w, keep_ref, row_block, col_block, nrow, ncol):
    width = ncol * BLOCK
    pieces = []
    for a in range(nrow):
        flags = [
            jnp.full((16, BLOCK), keep_ref[row_block + a, col_block + b].astype(jnp.float32))
            for b in range(ncol)
        ]
        flags = jnp.concatenate(flags, axis=1).astype(jnp.bfloat16)
        rows = w[a * BLOCK : (a + 1) * BLOCK, :].reshape(BLOCK // 16, 16, width)
        pieces.append((rows * flags[None]).reshape(BLOCK, width))
    return jnp.concatenate(pieces, axis=0)


def kernel(rows_n, cols_n, tok_in, gate_w, up_w, down_w, gate_k, up_k, down_k, out, *scratch):
    stages = cols_n.bit_length() - 1
    scratch = list(scratch)
    take = lambda n: [scratch.pop(0) for _ in range(n)]
    tok, gbuf, ubuf, dbuf, part, hid, acc, zsend, zrecv = take(9)
    got = take(stages)
    sent = [None] + take(stages - 1)
    wsem, tsend, trecv, zssem, zrsem, own_sem, rs_send, rs_recv, ag_send, ag_recv = take(10)

    chunks, total, width2 = part.shape
    width = width2 // 2
    local = tok_in.shape[0]
    feats = tok_in.shape[1]
    outs = down_w.shape[1]
    row = lax.axis_index("row")
    col = lax.axis_index("col")
    core = lax.rem(col, 2)

    partner, off, away = [], [0], []
    for j in range(stages):
        if j == 0:
            stride = 1
        else:
            stride = (1 - core) * (1 << j) + core * (1 << (stages - j))
        bit = lax.rem(lax.div(col, stride), 2)
        size = total >> (j + 1)
        partner.append(col + (1 - 2 * bit) * stride)
        away.append(off[j] + (1 - bit) * size)
        off.append(off[j] + bit * size)

    def rows_at(start, size):
        return pl.ds(pl.multiple_of(start, 16), size)

    def weights(c):
        s = lax.rem(c, SLOTS)
        cs = pl.ds(pl.multiple_of(c * width, BLOCK), width)
        return [
            pltpu.make_async_copy(gate_w.at[:, cs], gbuf.at[s], wsem.at[0, s]),
            pltpu.make_async_copy(up_w.at[:, cs], ubuf.at[s], wsem.at[1, s]),
        ]

    def downs(c):
        s = lax.rem(c, SLOTS)
        cs = pl.ds(pl.multiple_of(c * width, BLOCK), width)
        return pltpu.make_async_copy(down_w.at[cs, :], dbuf.at[s], wsem.at[2, s])

    def rs_copy(j, c):
        size = total >> (j + 1)
        src = part.at[c, rows_at(away[0], size)] if j == 0 else sent[j].at[c]
        return pltpu.make_async_remote_copy(
            src_ref=src, dst_ref=got[j].at[c], send_sem=rs_send.at[j, c],
            recv_sem=rs_recv.at[j, c], device_id=(row, partner[j]), device_id_type=MESH,
        )

    def ag_copy(j, c, start):
        view = hid.at[c, rows_at(start, total >> (j + 1))]
        return pltpu.make_async_remote_copy(
            src_ref=view, dst_ref=view, send_sem=ag_send.at[j, c],
            recv_sem=ag_recv.at[j, c], device_id=(row, partner[j]), device_id_type=MESH,
        )

    def tok_copy(i, start):
        return pltpu.make_async_remote_copy(
            src_ref=tok_in, dst_ref=tok.at[rows_at(start, local)], send_sem=tsend.at[i - 1],
            recv_sem=trecv.at[i - 1], device_id=(lax.rem(row + i, rows_n), col),
            device_id_type=MESH,
        )

    def z_copy(i):
        return pltpu.make_async_remote_copy(
            src_ref=zsend.at[i - 1], dst_ref=zrecv.at[i - 1], send_sem=zssem.at[i - 1],
            recv_sem=zrsem.at[i - 1], device_id=(lax.rem(row + i, rows_n), col),
            device_id_type=MESH,
        )

    for c in range(min(SLOTS - 1, chunks)):
        for copy in weights(c):
            copy.start()
        downs(c).start()
    own = pltpu.make_async_copy(tok_in, tok.at[rows_at(row * local, local)], own_sem)
    own.start()

    barrier = pltpu.get_barrier_semaphore()
    for j in range(stages):
        pl.semaphore_signal(barrier, inc=1, device_id=(row, partner[j]), device_id_type=MESH)
    for i in range(1, rows_n):
        pl.semaphore_signal(
            barrier, inc=1, device_id=(lax.rem(row + i, rows_n), col), device_id_type=MESH
        )
    pl.semaphore_wait(barrier, stages + rows_n - 1)

    for i in range(1, rows_n):
        tok_copy(i, row * local).start()
    acc[...] = jnp.zeros_like(acc)
    own.wait()
    for i in range(1, rows_n):
        tok_copy(i, lax.rem(row + rows_n - i, rows_n) * local).wait_recv()

    def expand(c):
        s = lax.rem(c, SLOTS)

        @pl.when(c + SLOTS - 1 < chunks)
        def _():
            for copy in weights(c + SLOTS - 1):
                copy.start()

        nb = width // BLOCK
        for copy, buf, keep, lo in zip(weights(c), (gbuf, ubuf), (gate_k, up_k), (0, width)):
            copy.wait()
            w = masked(buf[s], keep, 0, c * nb, feats // BLOCK, nb)
            part[c, :, lo : lo + width] = jnp.dot(
                tok[...], w, preferred_element_type=jnp.float32
            )
        rs_copy(0, c).start()

    def reduce_step(j, c):
        rs_copy(j, c).wait_recv()
        size = total >> (j + 1)
        if j < stages - 1:
            half = size // 2
            there = rows_at(away[j + 1], half)
            rel = rows_at(away[j + 1] - off[j + 1], half)
            sent[j + 1][c] = (part[c, there] + got[j][c, rel].astype(jnp.float32)).astype(
                jnp.bfloat16
            )
            rs_copy(j + 1, c).start()
            here = rows_at(off[j + 2], half)
            rel = rows_at(off[j + 2] - off[j + 1], half)
            part[c, here] = part[c, here] + got[j][c, rel].astype(jnp.float32)
        else:
            full = part[c, rows_at(off[stages], size)] + got[j][c].astype(jnp.float32)
            gate, up = full[:, :width], full[:, width:]
            hid[c, rows_at(off[stages], size)] = (gate / (1.0 + jnp.exp(-gate)) * up).astype(
                jnp.bfloat16
            )
            ag_copy(j, c, off[stages]).start()

    def gather_step(j, c):
        ag_copy(j, c, away[j]).wait_recv()
        ag_copy(j - 1, c, off[j]).start()

    def contract(c):
        s = lax.rem(c, SLOTS)

        @pl.when(c + SLOTS - 1 < chunks)
        def _():
            downs(c + SLOTS - 1).start()

        ag_copy(0, c, away[0]).wait_recv()
        downs(c).wait()
        nb = width // BLOCK
        w = masked(dbuf[s], down_k, c * nb, 0, nb, outs // BLOCK)
        acc[...] += jnp.dot(hid[c], w, preferred_element_type=jnp.float32)

    depth = 2 * stages
    line = [(LAG * (j + 1), functools.partial(reduce_step, j)) for j in range(stages)]
    line += [
        (LAG * (2 * stages - j), functools.partial(gather_step, j))
        for j in range(stages - 1, 0, -1)
    ]
    line += [(0, expand), (LAG * depth, contract)]

    def step(t, carry):
        for lag, work in line:
            if lag == 0:
                pl.when(t < chunks)(functools.partial(work, t))
            else:
                pl.when((t >= lag) & (t < chunks + lag))(functools.partial(work, t - lag))
        return carry

    lax.fori_loop(0, chunks + LAG * depth, step, 0)

    for i in range(1, rows_n):
        peer = lax.rem(row + i, rows_n)
        zsend[i - 1] = acc[rows_at(peer * local, local)].astype(jnp.bfloat16)
        z_copy(i).start()
    result = acc[rows_at(row * local, local)]
    for i in range(1, rows_n):
        z_copy(i).wait_recv()
        result = result + zrecv[i - 1].astype(jnp.float32)
    out[...] = result.astype(out.dtype)

    def drain(c, carry):
        for j in range(stages):
            rs_copy(j, c).wait_send()
            ag_copy(j, c, off[j + 1]).wait_send()
        return carry

    lax.fori_loop(0, chunks, drain, 0)
    for i in range(1, rows_n):
        tok_copy(i, row * local).wait_send()
        z_copy(i).wait_send()


def on_device(rows_n, cols_n, tokens, gate_w, up_w, down_w, gate_k, up_k, down_k):
    local, feats = tokens.shape
    units = gate_w.shape[1]
    outs = down_w.shape[1]
    total = local * rows_n
    width = min(WIDTH, units)
    chunks = units // width
    stages = cols_n.bit_length() - 1
    bf16, f32 = jnp.bfloat16, jnp.float32
    dma = pltpu.SemaphoreType.DMA
    scratch = [
        pltpu.VMEM((total, feats), bf16),
        pltpu.VMEM((SLOTS, feats, width), bf16),
        pltpu.VMEM((SLOTS, feats, width), bf16),
        pltpu.VMEM((SLOTS, width, outs), bf16),
        pltpu.VMEM((chunks, total, 2 * width), f32),
        pltpu.VMEM((chunks, total, width), bf16),
        pltpu.VMEM((total, outs), f32),
        pltpu.VMEM((rows_n - 1, local, outs), bf16),
        pltpu.VMEM((rows_n - 1, local, outs), bf16),
    ]
    for j in range(stages):
        scratch.append(
            pltpu.VMEM((chunks, total >> (j + 1), 2 * width), f32 if j == 0 else bf16)
        )
    for j in range(1, stages):
        scratch.append(pltpu.VMEM((chunks, total >> (j + 1), 2 * width), bf16))
    scratch += [
        dma((3, SLOTS)),
        dma((rows_n - 1,)),
        dma((rows_n - 1,)),
        dma((rows_n - 1,)),
        dma((rows_n - 1,)),
        dma,
        dma((stages, chunks)),
        dma((stages, chunks)),
        dma((stages, chunks)),
        dma((stages, chunks)),
    ]
    vmem = pl.BlockSpec(memory_space=pltpu.VMEM)
    smem = pl.BlockSpec(memory_space=pltpu.SMEM)
    hbm = pl.BlockSpec(memory_space=pl.ANY)
    flops = 6 * total * feats * units
    return pl.pallas_call(
        functools.partial(kernel, rows_n, cols_n),
        out_shape=jax.ShapeDtypeStruct((local, outs), bf16),
        in_specs=[vmem, hbm, hbm, hbm, smem, smem, smem],
        out_specs=vmem,
        scratch_shapes=scratch,
        compiler_params=pltpu.CompilerParams(
            collective_id=0, has_side_effects=True, vmem_limit_bytes=60 * 1024 * 1024
        ),
        cost_estimate=pl.CostEstimate(
            flops=flops, bytes_accessed=6 * feats * units, transcendentals=0
        ),
        name="swiglu",
    )(tokens, gate_w, up_w, down_w, gate_k, up_k, down_k)


def solution(mesh):
    placed = (
        P("row", "col"),
        P("col", "row"),
        P("col", "row"),
        P("row", "col"),
        P("col", "row"),
        P("col", "row"),
        P("row", "col"),
    )
    return jax.shard_map(
        functools.partial(on_device, mesh.shape["row"], mesh.shape["col"]),
        mesh=mesh, in_specs=placed, out_specs=P("row", "col"), check_vma=False,
    )
```

```python
import functools

import jax
import jax.numpy as jnp
from jax import lax
from jax.experimental import pallas as pl
from jax.experimental.pallas import tpu as pltpu
from jax.sharding import PartitionSpec as P

BLOCK = 128
WIDTH = 1024
PASSES = 2
LAG = 2
SLOTS = 3
MESH = pl.DeviceIdType.MESH


def masked(w, keep_ref, row_block, col_block, nrow, ncol):
    width = ncol * BLOCK
    pieces = []
    for a in range(nrow):
        flags = [
            jnp.full((16, BLOCK), keep_ref[row_block + a, col_block + b].astype(jnp.float32))
            for b in range(ncol)
        ]
        flags = jnp.concatenate(flags, axis=1).astype(jnp.bfloat16)
        rows = w[a * BLOCK : (a + 1) * BLOCK, :].reshape(BLOCK // 16, 16, width)
        pieces.append((rows * flags[None]).reshape(BLOCK, width))
    return jnp.concatenate(pieces, axis=0)


def kernel(rows_n, cols_n, tok_in, gate_w, up_w, down_w, gate_k, up_k, down_k, out, *scratch):
    stages = cols_n.bit_length() - 1
    scratch = list(scratch)
    take = lambda n: [scratch.pop(0) for _ in range(n)]
    tok, gbuf, ubuf, dbuf, part, hid, acc, zsend, zrecv = take(9)
    got = take(stages)
    sent = [None] + take(stages - 1)
    wsem, tsend, trecv, zssem, zrsem, own_sem, rs_send, rs_recv, ag_send, ag_recv = take(10)

    chunks, total, width2 = part.shape
    width = width2 // 2
    local = tok_in.shape[0] // PASSES
    per_pass = chunks // PASSES
    feats = tok_in.shape[1]
    outs = down_w.shape[1]
    row = lax.axis_index("row")
    col = lax.axis_index("col")
    core = lax.rem(col, 2)

    partner, off, away = [], [0], []
    for j in range(stages):
        if j == 0:
            stride = 1
        else:
            stride = (1 - core) * (1 << j) + core * (1 << (stages - j))
        bit = lax.rem(lax.div(col, stride), 2)
        size = total >> (j + 1)
        partner.append(col + (1 - 2 * bit) * stride)
        away.append(off[j] + (1 - bit) * size)
        off.append(off[j] + bit * size)

    def rows_at(start, size):
        return pl.ds(pl.multiple_of(start, 16), size)

    def weights(c):
        s = lax.rem(c, SLOTS)
        cs = pl.ds(pl.multiple_of(lax.rem(c, per_pass) * width, BLOCK), width)
        return [
            pltpu.make_async_copy(gate_w.at[:, cs], gbuf.at[s], wsem.at[0, s]),
            pltpu.make_async_copy(up_w.at[:, cs], ubuf.at[s], wsem.at[1, s]),
        ]

    def downs(c):
        s = lax.rem(c, SLOTS)
        cs = pl.ds(pl.multiple_of(lax.rem(c, per_pass) * width, BLOCK), width)
        return pltpu.make_async_copy(down_w.at[cs, :], dbuf.at[s], wsem.at[2, s])

    def rs_copy(j, c):
        size = total >> (j + 1)
        src = part.at[c, rows_at(away[0], size)] if j == 0 else sent[j].at[c]
        return pltpu.make_async_remote_copy(
            src_ref=src, dst_ref=got[j].at[c], send_sem=rs_send.at[j, c],
            recv_sem=rs_recv.at[j, c], device_id=(row, partner[j]), device_id_type=MESH,
        )

    def ag_copy(j, c, start):
        view = hid.at[c, rows_at(start, total >> (j + 1))]
        return pltpu.make_async_remote_copy(
            src_ref=view, dst_ref=view, send_sem=ag_send.at[j, c],
            recv_sem=ag_recv.at[j, c], device_id=(row, partner[j]), device_id_type=MESH,
        )

    def tok_copy(p, i, start):
        return pltpu.make_async_remote_copy(
            src_ref=tok_in.at[p * local : (p + 1) * local],
            dst_ref=tok.at[p, rows_at(start, local)],
            send_sem=tsend.at[p, i - 1], recv_sem=trecv.at[p, i - 1], device_id=(lax.rem(row + i, rows_n), col),
            device_id_type=MESH,
        )

    def z_copy(p, i):
        return pltpu.make_async_remote_copy(
            src_ref=zsend.at[p, i - 1], dst_ref=zrecv.at[p, i - 1], send_sem=zssem.at[p, i - 1],
            recv_sem=zrsem.at[p, i - 1], device_id=(lax.rem(row + i, rows_n), col),
            device_id_type=MESH,
        )

    for c in range(min(SLOTS - 1, chunks)):
        for copy in weights(c):
            copy.start()
        downs(c).start()
    own = [
        pltpu.make_async_copy(
            tok_in.at[p * local : (p + 1) * local],
            tok.at[p, rows_at(row * local, local)],
            own_sem.at[p],
        )
        for p in range(PASSES)
    ]
    for copy in own:
        copy.start()

    barrier = pltpu.get_barrier_semaphore()
    for j in range(stages):
        pl.semaphore_signal(barrier, inc=1, device_id=(row, partner[j]), device_id_type=MESH)
    for i in range(1, rows_n):
        pl.semaphore_signal(
            barrier, inc=1, device_id=(lax.rem(row + i, rows_n), col), device_id_type=MESH
        )
    pl.semaphore_wait(barrier, stages + rows_n - 1)

    def tokens_in(p):
        for i in range(1, rows_n):
            tok_copy(p, i, lax.rem(row + rows_n - i, rows_n) * local).wait_recv()
        if p + 1 < PASSES:
            for i in range(1, rows_n):
                tok_copy(p + 1, i, row * local).start()

    for i in range(1, rows_n):
        tok_copy(0, i, row * local).start()
    acc[...] = jnp.zeros_like(acc)
    for copy in own:
        copy.wait()
    tokens_in(0)

    def results_out(p):
        for i in range(1, rows_n):
            peer = lax.rem(row + i, rows_n)
            zsend[p, i - 1] = acc[p, rows_at(peer * local, local)].astype(jnp.bfloat16)
            z_copy(p, i).start()

    def expand(c):
        s = lax.rem(c, SLOTS)

        @pl.when(c + SLOTS - 1 < chunks)
        def _():
            for copy in weights(c + SLOTS - 1):
                copy.start()

        for p in range(1, PASSES):
            pl.when(c == p * per_pass)(functools.partial(tokens_in, p))

        nb = width // BLOCK
        first = lax.rem(c, per_pass) * nb
        for copy, buf, keep, lo in zip(weights(c), (gbuf, ubuf), (gate_k, up_k), (0, width)):
            copy.wait()
            w = masked(buf[s], keep, 0, first, feats // BLOCK, nb)
            part[c, :, lo : lo + width] = jnp.dot(
                tok[lax.div(c, per_pass)], w, preferred_element_type=jnp.float32
            )
        rs_copy(0, c).start()

    def reduce_step(j, c):
        rs_copy(j, c).wait_recv()
        size = total >> (j + 1)
        if j < stages - 1:
            half = size // 2
            there = rows_at(away[j + 1], half)
            rel = rows_at(away[j + 1] - off[j + 1], half)
            sent[j + 1][c] = (part[c, there] + got[j][c, rel].astype(jnp.float32)).astype(
                jnp.bfloat16
            )
            rs_copy(j + 1, c).start()
            here = rows_at(off[j + 2], half)
            rel = rows_at(off[j + 2] - off[j + 1], half)
            part[c, here] = part[c, here] + got[j][c, rel].astype(jnp.float32)
        else:
            full = part[c, rows_at(off[stages], size)] + got[j][c].astype(jnp.float32)
            gate, up = full[:, :width], full[:, width:]
            hid[c, rows_at(off[stages], size)] = (gate / (1.0 + jnp.exp(-gate)) * up).astype(
                jnp.bfloat16
            )
            ag_copy(j, c, off[stages]).start()

    def gather_step(j, c):
        ag_copy(j, c, away[j]).wait_recv()
        ag_copy(j - 1, c, off[j]).start()

    def contract(c):
        s = lax.rem(c, SLOTS)

        @pl.when(c + SLOTS - 1 < chunks)
        def _():
            downs(c + SLOTS - 1).start()

        ag_copy(0, c, away[0]).wait_recv()
        downs(c).wait()
        nb = width // BLOCK
        w = masked(dbuf[s], down_k, lax.rem(c, per_pass) * nb, 0, nb, outs // BLOCK)
        now = lax.div(c, per_pass)
        acc[now] = acc[now] + jnp.dot(hid[c], w, preferred_element_type=jnp.float32)
        for p in range(PASSES):
            pl.when(c == (p + 1) * per_pass - 1)(functools.partial(results_out, p))

    depth = 2 * stages
    line = [(LAG * (j + 1), functools.partial(reduce_step, j)) for j in range(stages)]
    line += [
        (LAG * (2 * stages - j), functools.partial(gather_step, j))
        for j in range(stages - 1, 0, -1)
    ]
    line += [(0, expand), (LAG * depth, contract)]

    def step(t, carry):
        for lag, work in line:
            if lag == 0:
                pl.when(t < chunks)(functools.partial(work, t))
            else:
                pl.when((t >= lag) & (t < chunks + lag))(functools.partial(work, t - lag))
        return carry

    lax.fori_loop(0, chunks + LAG * depth, step, 0)

    for p in range(PASSES):
        result = acc[p, rows_at(row * local, local)]
        for i in range(1, rows_n):
            z_copy(p, i).wait_recv()
            result = result + zrecv[p, i - 1].astype(jnp.float32)
        out[p * local : (p + 1) * local] = result.astype(out.dtype)

    def drain(c, carry):
        for j in range(stages):
            rs_copy(j, c).wait_send()
            ag_copy(j, c, off[j + 1]).wait_send()
        return carry

    lax.fori_loop(0, chunks, drain, 0)
    for p in range(PASSES):
        for i in range(1, rows_n):
            tok_copy(p, i, row * local).wait_send()
            z_copy(p, i).wait_send()


def on_device(rows_n, cols_n, tokens, gate_w, up_w, down_w, gate_k, up_k, down_k):
    local, feats = tokens.shape
    units = gate_w.shape[1]
    outs = down_w.shape[1]
    local = local // PASSES
    total = local * rows_n
    width = next(w for w in range(WIDTH, 0, -BLOCK) if units % w == 0)
    chunks = PASSES * (units // width)
    stages = cols_n.bit_length() - 1
    bf16, f32 = jnp.bfloat16, jnp.float32
    dma = pltpu.SemaphoreType.DMA
    scratch = [
        pltpu.VMEM((PASSES, total, feats), bf16),
        pltpu.VMEM((SLOTS, feats, width), bf16),
        pltpu.VMEM((SLOTS, feats, width), bf16),
        pltpu.VMEM((SLOTS, width, outs), bf16),
        pltpu.VMEM((chunks, total, 2 * width), f32),
        pltpu.VMEM((chunks, total, width), bf16),
        pltpu.VMEM((PASSES, total, outs), f32),
        pltpu.VMEM((PASSES, rows_n - 1, local, outs), bf16),
        pltpu.VMEM((PASSES, rows_n - 1, local, outs), bf16),
    ]
    for j in range(stages):
        scratch.append(
            pltpu.VMEM((chunks, total >> (j + 1), 2 * width), f32 if j == 0 else bf16)
        )
    for j in range(1, stages):
        scratch.append(pltpu.VMEM((chunks, total >> (j + 1), 2 * width), bf16))
    scratch += [
        dma((3, SLOTS)),
        dma((PASSES, rows_n - 1)),
        dma((PASSES, rows_n - 1)),
        dma((PASSES, rows_n - 1)),
        dma((PASSES, rows_n - 1)),
        dma((PASSES,)),
        dma((stages, chunks)),
        dma((stages, chunks)),
        dma((stages, chunks)),
        dma((stages, chunks)),
    ]
    vmem = pl.BlockSpec(memory_space=pltpu.VMEM)
    smem = pl.BlockSpec(memory_space=pltpu.SMEM)
    hbm = pl.BlockSpec(memory_space=pl.ANY)
    flops = 6 * PASSES * total * feats * units
    return pl.pallas_call(
        functools.partial(kernel, rows_n, cols_n),
        out_shape=jax.ShapeDtypeStruct((PASSES * local, outs), bf16),
        in_specs=[vmem, hbm, hbm, hbm, smem, smem, smem],
        out_specs=vmem,
        scratch_shapes=scratch,
        compiler_params=pltpu.CompilerParams(
            collective_id=0, has_side_effects=True, vmem_limit_bytes=60 * 1024 * 1024
        ),
        cost_estimate=pl.CostEstimate(
            flops=flops, bytes_accessed=6 * feats * units, transcendentals=0
        ),
        name="swiglu",
    )(tokens, gate_w, up_w, down_w, gate_k, up_k, down_k)


def solution(mesh):
    placed = (
        P("row", "col"),
        P("col", "row"),
        P("col", "row"),
        P("row", "col"),
        P("col", "row"),
        P("col", "row"),
        P("row", "col"),
    )
    return jax.shard_map(
        functools.partial(on_device, mesh.shape["row"], mesh.shape["col"]),
        mesh=mesh, in_specs=placed, out_specs=P("row", "col"), check_vma=False,
    )
```
